256 devices in a mesh: frame: 32 (over y_hi, z, core), patch: 8 (over x, y_lo).
Axes of the slice: x: 4, y: 4 (y_hi: 2, y_lo: 2; y = y_hi * 2 + y_lo), z: 8, core: 2. Of those that a mesh axis runs over, the one named last changes fastest.
Arguments:
- tokens: bfloat16 [128, 1024, 1280], P('frame', 'patch'), may hold values from -6 to 6
- spatial_in: bfloat16 [1280, 1920], replicated, may hold values from -1 to 1
- spatial_out: bfloat16 [640, 1280], replicated, may hold values from -0.25 to 0.25
- temporal_in: bfloat16 [1280, 1920], P('frame'), may hold values from -1 to 1
- temporal_out: bfloat16 [640, 1280], P('frame'), may hold values from -0.25 to 0.25
- spatial_gain: float32 [1280], replicated, may hold values from 0.1 to 1.9
- temporal_gain: float32 [1280], replicated, may hold values from 0.1 to 1.9
- keep_masks: int32 [8, 2], replicated, may hold values from 0 to 1, as said below
Outputs:
- layer_out: bfloat16 [128, 1024, 1280], P('frame', 'patch')
The draws below stay inside these ranges and needn't reach their ends.
Inputs may be any that keep to these rules, and one draw needn't show every extreme that they name: `keep_masks`: 1 keeps a video's branch, 0 drops it; in each branch at least one video keeps it and at least one drops it.
All inputs are finite; a program needn't handle non-finite values.
Results may differ from the reference program's by a relative error of at most 0.01.
Values may be sent and summed in bfloat16 or wider, within the bound.
A program may use at most 128 MiB of HBM per device.

```python
import jax
import jax.numpy as jnp
from jax import lax

D = 1280
HEADS = 8
HDIM = 80
PATCHES = 1024
CLIP_LEN = 16
FRAMES = 128
VIDEOS = 8


def projection_weight(key):
    base_weight = jnp.clip(jax.random.normal(key, (D, 3 * HEADS * HDIM), jnp.float32), -5.0, 5.0) * D ** (-0.5)
    return base_weight


def draw_tokens(key, part):
    key = jax.random.fold_in(key, 3)
    noise_key = jax.random.fold_in(key, 0)
    return jnp.clip(jax.random.normal(noise_key, (FRAMES, PATCHES, D), jnp.float32), -6.0, 6.0).astype(jnp.bfloat16)


def draw_spatial_in(key, part):
    key = jax.random.fold_in(key, 5)
    return projection_weight(key).astype(jnp.bfloat16)


def draw_temporal_in(key, part):
    key = jax.random.fold_in(key, 7)
    return projection_weight(key).astype(jnp.bfloat16)


def draw_keep_masks(key, part):
    key = jax.random.fold_in(key, 11)
    bits_key, first_key, second_key = jax.random.split(key, 3)
    flags = jax.random.randint(bits_key, (VIDEOS, 2), 0, 2).astype(jnp.int32)
    order_one = jax.random.permutation(first_key, VIDEOS)
    order_two = jax.random.permutation(second_key, VIDEOS)
    flags = flags.at[order_one[0], 0].set(1).at[order_one[1], 0].set(0)
    flags = flags.at[order_two[0], 1].set(1).at[order_two[1], 1].set(0)
    return flags


def level_of(rng, dims, cuts, low, top_value):
    def one(position, parts):
        draws = jax.random.uniform(jax.random.fold_in(jax.random.fold_in(rng, 6), position), (parts,), jnp.float32, low / len(cuts), top_value / len(cuts))
        return jnp.repeat(jnp.exp(draws), dims[position] // parts).reshape((-1,) + (1,) * (len(dims) - position - 1))

    level = one(*cuts[0])
    for cut in cuts[1:]:
        level = level * one(*cut)
    return level


def noise(stream_key, shape, scale, limit, cuts=(), kind=jnp.bfloat16):
    factor_of = level_of(stream_key, shape, cuts, -0.22, 0.18) if cuts else 1.0
    drawn = jax.random.normal(stream_key, shape, jnp.float32) * scale * factor_of
    return jnp.minimum(jnp.maximum(drawn, -limit), limit).astype(kind)


def setup_inputs(seed: int = 0) -> dict:
    streams_of = jax.random.split(jax.random.key(seed), 9)
    tokens = draw_tokens(jax.random.fold_in(streams_of[8], 71), 0)
    spatial_in = draw_spatial_in(jax.random.fold_in(streams_of[8], 71), 0)
    spatial_out = noise(streams_of[2], (HEADS * HDIM, D), (HEADS * HDIM) ** -0.5, 0.25)
    temporal_in = draw_temporal_in(jax.random.fold_in(streams_of[8], 71), 0)
    temporal_out = noise(streams_of[4], (HEADS * HDIM, D), (HEADS * HDIM) ** -0.5, 0.25, ((0, 32),))
    spatial_gain = jnp.clip(1.0 + 0.18 * jax.random.normal(streams_of[5], (D,), jnp.float32), 0.1, 1.9)
    temporal_gain = jnp.clip(1.0 + 0.18 * jax.random.normal(streams_of[6], (D,), jnp.float32), 0.1, 1.9)
    keep_masks = draw_keep_masks(jax.random.fold_in(streams_of[8], 71), 0)
    return {"tokens": tokens, "spatial_in": spatial_in, "spatial_out": spatial_out, "temporal_in": temporal_in, "temporal_out": temporal_out, "spatial_gain": spatial_gain, "temporal_gain": temporal_gain, "keep_masks": keep_masks}


keep_rate = 0.7

def normalize(values, gain):
    values = values.astype(jnp.float32)
    center = lax.optimization_barrier(jnp.mean(values, axis=-1, keepdims=True))
    spread = lax.optimization_barrier(jnp.mean(jnp.square(values - center), axis=-1, keepdims=True))
    return ((values - center) * lax.rsqrt(spread + 1e-06) * gain).astype(jnp.bfloat16)

def reference(tokens, spatial_in, spatial_out, temporal_in, temporal_out, spatial_gain, temporal_gain, keep_masks):
    inner = HEADS * HDIM
    factor = HDIM ** (-0.5)
    coef_space = jnp.repeat(keep_masks[:, 0].astype(jnp.float32) / keep_rate, CLIP_LEN)
    coef_time = keep_masks[:, 1].astype(jnp.float32) / keep_rate

    def spatial_frame(packed):
        frame_tokens, branch_coef = packed
        normed = normalize(frame_tokens, spatial_gain)
        triple = jnp.dot(normed, spatial_in, preferred_element_type=jnp.float32).astype(jnp.bfloat16)
        triple = triple.reshape(PATCHES, 3, HEADS, HDIM).astype(jnp.float32)
        scores = jnp.einsum('qhd,khd->hqk', triple[:, 0], triple[:, 1]) * factor
        chances = jax.nn.softmax(scores, axis=-1).astype(jnp.bfloat16).astype(jnp.float32)
        mixed = jnp.einsum('hqk,khd->qhd', chances, triple[:, 2]).astype(jnp.bfloat16).reshape(PATCHES, inner)
        projected = jnp.dot(mixed, spatial_out, preferred_element_type=jnp.float32)
        return (frame_tokens.astype(jnp.float32) + branch_coef * projected).astype(jnp.bfloat16)
    after_space = lax.map(spatial_frame, (tokens, coef_space))

    def temporal_video(packed):
        video_tokens, branch_coef = packed
        normed = normalize(video_tokens, temporal_gain).reshape(CLIP_LEN * PATCHES, D)
        triple = jnp.dot(normed, temporal_in, preferred_element_type=jnp.float32).astype(jnp.bfloat16)
        triple = triple.reshape(CLIP_LEN, PATCHES, 3, HEADS, HDIM).astype(jnp.float32)
        scores = jnp.einsum('fphd,gphd->phfg', triple[:, :, 0], triple[:, :, 1]) * factor
        chances = jax.nn.softmax(scores, axis=-1).astype(jnp.bfloat16).astype(jnp.float32)
        mixed = jnp.einsum('phfg,gphd->fphd', chances, triple[:, :, 2]).astype(jnp.bfloat16)
        projected = jnp.dot(mixed.reshape(CLIP_LEN * PATCHES, inner), temporal_out, preferred_element_type=jnp.float32)
        projected = projected.reshape(CLIP_LEN, PATCHES, D)
        return (video_tokens.astype(jnp.float32) + branch_coef * projected).astype(jnp.bfloat16)
    grouped = after_space.reshape(VIDEOS, CLIP_LEN, PATCHES, D)
    result = lax.map(temporal_video, (grouped, coef_time))
    return result.reshape(VIDEOS * CLIP_LEN, PATCHES, D)
```

```python
import jax
import jax.numpy as jnp
from jax import lax
from jax.experimental import pallas as pl
from jax.experimental.pallas import tpu as pltpu
from jax.sharding import PartitionSpec as P

MESH = pl.DeviceIdType.MESH
BF = jnp.bfloat16
F32 = jnp.float32

HEADS = 8
HDIM = 80
INNER = HEADS * HDIM
D = 1280
KEEP = 0.7
EXP_SCALE = HDIM ** (-0.5) * 1.4426950408889634


def flip(a, b):
    return (a + b) % 2


def flip_x(x, key):
    low, high = x % 2, x // 2
    if key % 2:
        low = 1 - low
    if key // 2:
        high = 1 - high
    return 2 * high + low


def layer_norm(x, gain):
    center = jnp.sum(x, axis=-1, keepdims=True) * (1.0 / D)
    x = x - center
    spread = jnp.sum(x * x, axis=-1, keepdims=True) * (1.0 / D)
    return (x * lax.rsqrt(spread + 1e-06) * gain).astype(BF)


def dot(a, b):
    return jnp.dot(a, b, preferred_element_type=F32)


def dot_t(a, b):
    return lax.dot_general(a, b, (((1,), (1,)), ((), ())), preferred_element_type=F32)


def pick(rows, columns, group, stride):
    r = lax.broadcasted_iota(jnp.int32, (rows, columns), 0)
    c = lax.broadcasted_iota(jnp.int32, (rows, columns), 1)
    block = jnp.zeros_like(r)
    for n in range(1, (rows + group - 1) // group):
        block = block + (r >= n * group).astype(jnp.int32)
    hit = (c == r + block * (stride - group)) & (r < group * (columns // stride))
    return jnp.where(hit, 1.0, 0.0).astype(BF)


def layer(
    tok_hbm, swin_hbm, swout_hbm, tin_sh, tout_sh, sgain, tgain, keep, out_hbm,
    tok, swin, swout, twin, gout, twout, raw_in_st, raw_out_st, raw_in, raw_out,
    xin, q_s, k_s, v_s, o_s, mx, mback, asp, tin, tm, tb, out_v, bias,
    load_sem, tok_send, tok_recv, kv_send, kv_recv, mx_send, mx_recv,
    as_send, as_recv, tm_send, tm_recv, raw_send, raw_recv,
    ring_send, ring_recv, sib_send, sib_recv, out_sem,
):
    f = lax.axis_index("frame")
    p = lax.axis_index("patch")
    c = f % 2
    z = (f // 2) % 8
    yh = f // 16
    x = p // 2
    yl = p % 2
    fbase = f - c
    video = f // 4
    g = f % 4
    zb = z % 2
    sib = fbase + 1 - c

    def remote(src, dst, send, recv, frame, patch):
        return pltpu.make_async_remote_copy(
            src_ref=src, dst_ref=dst, send_sem=send, recv_sem=recv,
            device_id=(frame, patch), device_id_type=MESH)

    def wait_in(dst, sem):
        pltpu.make_async_copy(dst, dst, sem).wait()

    wait_out = wait_in

    loads = [
        pltpu.make_async_copy(tok_hbm, tok, load_sem.at[0]),
        pltpu.make_async_copy(swin_hbm, swin, load_sem.at[1]),
        pltpu.make_async_copy(swout_hbm, swout, load_sem.at[2]),
    ]

    barrier = pltpu.get_barrier_semaphore()

    def greet(frame, patch):
        pl.semaphore_signal(barrier, inc=1, device_id=(frame, patch), device_id_type=MESH)

    zother = (z + 7 + 2 * zb) % 8
    yflip = (f + 16) % 32 - c
    for n in range(4):
        for b in range(2):
            patch = 2 * flip_x(x, n) + flip(yl, b)
            greet(sib, patch)
            if n or b:
                greet(f, patch)
    zpair = (f - g) + 2 * (1 - zb)
    greet(zpair, p)
    greet(zpair + 1, p)
    greet(yh * 16 + 2 * zother + c, p)
    greet(yflip, 2 * x + 1 - yl)
    greet(yflip + 1, 2 * x + 1 - yl)
    loads[1].start()
    raw_in_st[...] = jnp.zeros_like(raw_in_st)
    raw_out_st[...] = jnp.zeros_like(raw_out_st)
    raw_in_st[0:40, :] = tin_sh[...]
    raw_out_st[0:20, :] = tout_sh[...]
    q_s[...] = jnp.zeros_like(q_s)
    k_s[:, 0:512, :] = jnp.zeros((HEADS, 512, 128), BF)
    lane = lax.broadcasted_iota(jnp.int32, (HEADS, 512, 128), 2)
    v_s[:, 0:512, :] = jnp.where(lane == HDIM, 1.0, 0.0).astype(BF)
    rr = lax.broadcasted_iota(jnp.int32, (256, 256), 0) % 16
    cc = lax.broadcasted_iota(jnp.int32, (256, 256), 1) % 16
    bias[...] = jnp.where(rr == cc, 0.0, -1e30).astype(F32)
    pl.semaphore_wait(barrier, 20)

    yc = flip(yl, c)
    for n in (3, 1, 2, 0):
        key = n ^ (n >> 1)
        xd = flip_x(x, key)
        for hh in (1, 0):
            half = flip(c, hh)
            src = tok_hbm.at[xd, pl.ds(4 * half, 4)]
            dst = xin.at[2 * n + yc]
            idx = 2 * n + hh
            move = remote(src, dst, tok_send.at[idx], tok_recv.at[2 * n + yc], fbase + half, 2 * xd + c)
            if n == 0 and hh == 0:
                @pl.when(yc == 0)
                def _():
                    pltpu.make_async_copy(src, dst, tok_recv.at[0]).start()

                @pl.when(yc != 0)
                def _():
                    move.start()
            else:
                move.start()

    for a, (st, raw) in enumerate(((raw_in_st, raw_in), (raw_out_st, raw_out))):
        remote(st, raw.at[c], raw_send.at[0, a], raw_recv.at[c, a], yflip + 1, 2 * x + 1 - yl).start()

        @pl.when(c == 0)
        def _():
            pltpu.make_async_copy(st, raw.at[0], raw_recv.at[0, a]).start()

        @pl.when(c != 0)
        def _():
            remote(st, raw.at[1], raw_send.at[1, a], raw_recv.at[1, a], fbase, p).start()
    loads[0].start()
    loads[2].start()

    yh_unit = flip(yh, c)
    toward = 1 - 2 * c

    def unit_at(offset):
        return yh_unit * 8 + (z + offset + 16) % 8

    def unit_refs(u):
        return (twin.at[pl.ds(pl.multiple_of(u * 80, 16), 80)], gout.at[u])

    def ring(way, step):
        sign = toward if way == 0 else -toward
        u = unit_at(-sign * (step - 1))
        frame = yh * 16 + 2 * ((z + sign + 8) % 8) + c
        return [
            remote(r, r, ring_send.at[way, step - 1, a], ring_recv.at[way, step - 1, a], frame, p)
            for a, r in enumerate(unit_refs(u))
        ]

    def ring_arrived(way, step):
        sign = toward if way == 0 else -toward
        u = unit_at(-sign * step)
        for a, r in enumerate(unit_refs(u)):
            wait_in(r, ring_recv.at[way, step - 1, a])
        return u

    def share(u, label):
        for a, r in enumerate(unit_refs(u)):
            remote(r, r, sib_send.at[label, a], sib_recv.at[label, a], sib, p).start()

    def weights_begin():
        for a, raw in enumerate((raw_in, raw_out)):
            wait_in(raw.at[0], raw_recv.at[0, a])
            wait_in(raw.at[1], raw_recv.at[1, a])
        u = unit_at(0)
        twin[pl.ds(pl.multiple_of(u * 80, 16), 80), :] = dot(
            pick(80, 96, 40, 48), raw_in[...].reshape(96, 1920)).astype(BF)
        gout[u] = dot(pick(48, 64, 20, 32), raw_out[...].reshape(64, 1280)).astype(BF)
        for way in (0, 1):
            for m in ring(way, 1):
                m.start()
        share(u, 0)

    def weights_step(step):
        for way in (0, 1):
            if way == 1 and step == 4:
                continue
            u = ring_arrived(way, step)
            if step < (4 if way == 0 else 3):
                for m in ring(way, step + 1):
                    m.start()
            share(u, step if way == 0 else 4 + step)

    def weights_end():
        weights_step(4)
        other = flip(yh_unit, 1)
        for label in range(8):
            for a, r in enumerate(unit_refs(other * 8 + label)):
                wait_in(r, sib_recv.at[label, a])
        twout[...] = dot(pick(640, 768, 40, 48), gout[...].reshape(768, 1280)).astype(BF)

    loads[1].wait()

    def chunk(n, carry):
        @pl.when(n == 1)
        def _():
            weights_begin()

        for b in range(2):
            wait_in(xin.at[2 * n + b], tok_recv.at[2 * n + b])
        rows = xin[pl.ds(2 * n, 2)].reshape(128, D).astype(F32)
        triple = dot(layer_norm(rows, sgain[...]), swin[...]).astype(BF)
        at = pl.multiple_of(n * 128, 128)
        for h in range(HEADS):
            lo = h * HDIM
            k_s[h, pl.ds(at, 128), 0:HDIM] = triple[:, INNER + lo:INNER + lo + HDIM]
            v_s[h, pl.ds(at, 128), 0:HDIM] = triple[:, 2 * INNER + lo:2 * INNER + lo + HDIM]
        for a, r in enumerate((k_s, v_s)):
            remote(r.at[:, pl.ds(at, 128)], r.at[:, pl.ds(at + 512, 128)],
                   kv_send.at[n, a], kv_recv.at[n, a], sib, p).start()
        for h in range(HEADS):
            lo = h * HDIM
            for b in range(2):
                for j in range(2):
                    at_row = (2 * b + j) * 32
                    q_s[h, j, 2 * n + b, :, 0:HDIM] = triple[at_row:at_row + 32, lo:lo + HDIM]
        return carry

    lax.fori_loop(0, 4, chunk, 0)
    for n in range(4):
        for a, r in enumerate((k_s, v_s)):
            wait_in(r.at[:, pl.ds(n * 128 + 512, 128)], kv_recv.at[n, a])

    def attend(j):
        def head(h, carry):
            q = q_s[h, j].reshape(256, 128)
            s = dot_t(q, k_s[h])
            top = jnp.max(s, axis=-1, keepdims=True)
            e = jnp.exp2((s - top) * EXP_SCALE).astype(BF)
            o = dot(e, v_s[h])
            o_s[h] = (o * (1.0 / o[:, HDIM:HDIM + 1])).astype(BF)
            return carry

        lax.fori_loop(0, HEADS, head, 0)
        mixed = jnp.concatenate([o_s[h][:, 0:HDIM] for h in range(HEADS)], axis=1)
        mx[j] = mixed.reshape(8, 2, 16, INNER)
        for s in (7, 6, 5, 4, 3, 2, 1, 0):
            n, b = s // 2, s % 2
            key = n ^ (n >> 1)
            patch = 2 * flip_x(x, key) + flip(yl, b)
            src = mx.at[j, s]
            dst = mback.at[j, pl.ds(2 * c, 2), x]
            move = remote(src, dst, mx_send.at[j, s], mx_recv.at[j, 2 * x + c], fbase + yl, patch)
            if s == 0:
                @pl.when(yc == 0)
                def _():
                    pltpu.make_async_copy(src, dst, mx_recv.at[j, 2 * x + c]).start()

                @pl.when(yc != 0)
                def _():
                    move.start()
            else:
                move.start()

    coef_space = keep[video, 0].astype(F32) / KEEP
    coef_time = keep[video, 1].astype(F32) / KEEP

    def group_of(o, j):
        return (o // 2) * 4 + j * 2 + o % 2

    def after_space(j):
        for i in range(4):
            for h in range(2):
                wait_in(mback.at[j, pl.ds(2 * h, 2), i], mx_recv.at[j, 2 * i + h])
        y = dot(mback[j].reshape(256, INNER), swout[...])
        for o in range(4):
            for i in range(4):
                at = (4 * o + i) * 16
                asp[j, o, i] = (tok[i, group_of(o, j)].astype(F32) + coef_space * y[at:at + 16]).astype(BF)
        for k in (3, 2, 1, 0):
            o = 2 * flip(g // 2, k // 2) + flip(c, k % 2)
            src, dst = asp.at[j, o], tin.at[j, g]
            if k == 0:
                pltpu.make_async_copy(src, dst, as_recv.at[j, g]).start()
            else:
                remote(src, dst, as_send.at[j, k], as_recv.at[j, g], 4 * video + o, p).start()

    def temporal(j):
        rows = tin[j].reshape(256, D).astype(F32)
        triple = dot(layer_norm(rows, tgain[...]), twin[...]).astype(BF)
        parts = []
        for h in range(HEADS):
            lo = h * HDIM
            s = dot_t(triple[:, lo:lo + HDIM], triple[:, INNER + lo:INNER + lo + HDIM]) + bias[...]
            top = jnp.max(s, axis=-1, keepdims=True)
            e = jnp.exp2((s - top) * EXP_SCALE)
            total = jnp.sum(e, axis=-1, keepdims=True)
            o = dot(e.astype(BF), triple[:, 2 * INNER + lo:2 * INNER + lo + HDIM])
            parts.append((o * (1.0 / total)).astype(BF))
        tm[j] = jnp.concatenate(parts, axis=1).reshape(4, 64, INNER)
        for k in (3, 2, 1, 0):
            o = 2 * flip(g // 2, k // 2) + flip(c, k % 2)
            src, dst = tm.at[j, o], tb.at[j, g]
            if k == 0:
                pltpu.make_async_copy(src, dst, tm_recv.at[j, g]).start()
            else:
                remote(src, dst, tm_send.at[j, k], tm_recv.at[j, g], 4 * video + o, p).start()

    def finish(j):
        for o in range(4):
            wait_in(tb.at[j, o], tm_recv.at[j, o])
        y = dot(tb[j].reshape(256, INNER), twout[...])
        for o in range(4):
            for i in range(4):
                at = (4 * o + i) * 16
                out_v[i, group_of(o, j)] = (asp[j, o, i].astype(F32) + coef_time * y[at:at + 16]).astype(BF)
        for h in range(2):
            part = pl.ds(4 * h + 2 * j, 2)
            pltpu.make_async_copy(out_v.at[:, part], out_hbm.at[:, part], out_sem.at[j, h]).start()

    weights_step(1)
    attend(0)
    weights_step(2)
    attend(1)
    loads[0].wait()
    loads[2].wait()
    after_space(0)
    weights_step(3)
    after_space(1)
    weights_end()
    for j in range(2):
        for o in range(4):
            wait_in(tin.at[j, o], as_recv.at[j, o])
        temporal(j)
    for j in range(2):
        finish(j)

    for n in range(4):
        for hh in range(2):
            part = tok_hbm.at[0, pl.ds(0, 4)]
            if n == 0 and hh == 0:
                @pl.when(yc != 0)
                def _():
                    wait_out(part, tok_send.at[0])
            else:
                wait_out(part, tok_send.at[2 * n + hh])
    for n in range(4):
        for a, r in enumerate((k_s, v_s)):
            wait_out(r.at[:, pl.ds(n * 128, 128)], kv_send.at[n, a])
    for j in range(2):
        for s in range(8):
            if s == 0:
                @pl.when(yc != 0)
                def _():
                    wait_out(mx.at[j, s], mx_send.at[j, s])
            else:
                wait_out(mx.at[j, s], mx_send.at[j, s])
        for k in range(1, 4):
            wait_out(asp.at[j, k], as_send.at[j, k])
            wait_out(tm.at[j, k], tm_send.at[j, k])
    for a, st in enumerate((raw_in_st, raw_out_st)):
        wait_out(st, raw_send.at[0, a])

        @pl.when(c != 0)
        def _():
            wait_out(st, raw_send.at[1, a])
    for a, r in enumerate(unit_refs(0)):
        for way in range(2):
            for step in range(4 - way):
                wait_out(r, ring_send.at[way, step, a])
        for label in range(8):
            wait_out(r, sib_send.at[label, a])
    for j in range(2):
        for h in range(2):
            part = pl.ds(4 * h + 2 * j, 2)
            pltpu.make_async_copy(out_v.at[:, part], out_hbm.at[:, part], out_sem.at[j, h]).wait()


def on_device(tokens, spatial_in, spatial_out, temporal_in, temporal_out, spatial_gain, temporal_gain, keep_masks):
    dma = pltpu.SemaphoreType.DMA
    scratch = [
        pltpu.VMEM((4, 8, 16, D), BF),
        pltpu.VMEM((D, 3 * INNER), BF),
        pltpu.VMEM((INNER, D), BF),
        pltpu.VMEM((D, 3 * INNER), BF),
        pltpu.VMEM((16, 48, D), BF),
        pltpu.VMEM((INNER, D), BF),
        pltpu.VMEM((48, 3 * INNER), BF),
        pltpu.VMEM((32, D), BF),
        pltpu.VMEM((2, 48, 3 * INNER), BF),
        pltpu.VMEM((2, 32, D), BF),
        pltpu.VMEM((8, 4, 16, D), BF),
        pltpu.VMEM((HEADS, 2, 8, 32, 128), BF),
        pltpu.VMEM((HEADS, 1024, 128), BF),
        pltpu.VMEM((HEADS, 1024, 128), BF),
        pltpu.VMEM((HEADS, 256, 128), BF),
        pltpu.VMEM((2, 8, 2, 16, INNER), BF),
        pltpu.VMEM((2, 4, 4, 16, INNER), BF),
        pltpu.VMEM((2, 4, 4, 16, D), BF),
        pltpu.VMEM((2, 4, 4, 16, D), BF),
        pltpu.VMEM((2, 4, 64, INNER), BF),
        pltpu.VMEM((2, 4, 64, INNER), BF),
        pltpu.VMEM((4, 8, 16, D), BF),
        pltpu.VMEM((256, 256), F32),
        dma((3,)), dma((8,)), dma((8,)), dma((4, 2)), dma((4, 2)), dma((2, 8)), dma((2, 8)),
        dma((2, 4)), dma((2, 4)), dma((2, 4)), dma((2, 4)), dma((2, 2)), dma((2, 2)),
        dma((2, 4, 2)), dma((2, 4, 2)), dma((8, 2)), dma((8, 2)), dma((2, 2)),
    ]
    any_space = pl.BlockSpec(memory_space=pl.ANY)
    vmem = pl.BlockSpec(memory_space=pltpu.VMEM)
    out = pl.pallas_call(
        layer,
        out_shape=jax.ShapeDtypeStruct((4, 8, 16, D), BF),
        in_specs=[any_space, any_space, any_space, vmem, vmem, vmem, vmem,
                  pl.BlockSpec(memory_space=pltpu.SMEM)],
        out_specs=any_space,
        scratch_shapes=scratch,
        compiler_params=pltpu.CompilerParams(
            collective_id=0, has_side_effects=True, vmem_limit_bytes=60 * 1024 * 1024),
    )(tokens.reshape(4, 8, 16, D), spatial_in, spatial_out, temporal_in, temporal_out,
      spatial_gain.reshape(1, D), temporal_gain.reshape(1, D), keep_masks)
    return out.reshape(4, 128, D)


def solution(mesh):
    placed = (
        P("frame", "patch", None), P(), P(), P("frame", None), P("frame", None), P(), P(), P(),
    )
    return jax.shard_map(
        on_device, mesh=mesh, in_specs=placed, out_specs=P("frame", "patch", None), check_vma=False)
```

```python
import jax
import jax.numpy as jnp
from jax import lax
from jax.experimental import pallas as pl
from jax.experimental.pallas import tpu as pltpu
from jax.sharding import PartitionSpec as P

MESH = pl.DeviceIdType.MESH
BF = jnp.bfloat16
F32 = jnp.float32

HEADS = 8
HDIM = 80
INNER = HEADS * HDIM
D = 1280
KEEP = 0.7
UNROLL = 4
SERVICE = ((0, ((0, 1), (1, 1)), ()), (2, ((0, 2), (1, 2)), (0,)))
PLAN = (
    ('attend', 0, 1),
    ('core1', 1),
    ('core0', (0, 3), (1, 3)),
    ('attend', 1, 1),
    ('after', 0),
    ('core1', 2),
    ('attend', 2, 1),
    ('after', 1),
    ('core0', (0, 4)),
    ('attend', 3, 1),
    ('core1', 3),
    ('after', 2),
    ('after', 3),
    ('end',),
    ('temporal', 0, 2),
    ('temporal', 2, 2),
    ('finish', 0, 2),
    ('finish', 2, 2),
)
EXP_SCALE = HDIM ** (-0.5) * 1.4426950408889634


def flip(a, b):
    return (a + b) % 2


def flip_x(x, key):
    low, high = x % 2, x // 2
    if key % 2:
        low = 1 - low
    if key // 2:
        high = 1 - high
    return 2 * high + low


def layer_norm(x, gain):
    center = jnp.sum(x, axis=-1, keepdims=True) * (1.0 / D)
    x = x - center
    spread = jnp.sum(x * x, axis=-1, keepdims=True) * (1.0 / D)
    return (x * lax.rsqrt(spread + 1e-06) * gain).astype(BF)


def dot(a, b):
    return jnp.dot(a, b, preferred_element_type=F32)


def dot_t(a, b):
    return lax.dot_general(a, b, (((1,), (1,)), ((), ())), preferred_element_type=F32)


def pick(rows, columns, group, stride):
    r = lax.broadcasted_iota(jnp.int32, (rows, columns), 0)
    c = lax.broadcasted_iota(jnp.int32, (rows, columns), 1)
    block = jnp.zeros_like(r)
    for n in range(1, (rows + group - 1) // group):
        block = block + (r >= n * group).astype(jnp.int32)
    hit = (c == r + block * (stride - group)) & (r < group * (columns // stride))
    return jnp.where(hit, 1.0, 0.0).astype(BF)


def layer(
    tok_hbm, swin_hbm, swout_hbm, tin_sh, tout_sh, sgain, tgain, keep, out_hbm,
    tok, swin, swout, twin, gout, twout, raw_in_st, raw_out_st, raw_in, raw_out,
    xin, q_s, k_s, v_s, o_s, mx, mback, asp, tin, tm, tb, out_v, bias,
    load_sem, tok_send, tok_recv, kv_send, kv_recv, mx_send, mx_recv,
    as_send, as_recv, tm_send, tm_recv, raw_send, raw_recv,
    ring_send, ring_recv, sib_send, sib_recv, lend_send, lend_recv, out_sem,
):
    f = lax.axis_index("frame")
    p = lax.axis_index("patch")
    c = f % 2
    z = (f // 2) % 8
    yh = f // 16
    x = p // 2
    yl = p % 2
    fbase = f - c
    video = f // 4
    g = f % 4
    zb = z % 2
    sib = fbase + 1 - c

    def remote(src, dst, send, recv, frame, patch):
        return pltpu.make_async_remote_copy(
            src_ref=src, dst_ref=dst, send_sem=send, recv_sem=recv,
            device_id=(frame, patch), device_id_type=MESH)

    def wait_in(dst, sem):
        pltpu.make_async_copy(dst, dst, sem).wait()

    wait_out = wait_in

    loads = [
        pltpu.make_async_copy(tok_hbm, tok, load_sem.at[0]),
        pltpu.make_async_copy(swin_hbm, swin, load_sem.at[1]),
        pltpu.make_async_copy(swout_hbm, swout, load_sem.at[2]),
    ]

    barrier = pltpu.get_barrier_semaphore()

    def greet(frame, patch):
        pl.semaphore_signal(barrier, inc=1, device_id=(frame, patch), device_id_type=MESH)

    zother = (z + 7 + 2 * zb) % 8
    yflip = (f + 16) % 32 - c
    for n in range(4):
        for b in range(2):
            patch = 2 * flip_x(x, n) + flip(yl, b)
            greet(sib, patch)
            if n or b:
                greet(f, patch)
    zpair = (f - g) + 2 * (1 - zb)
    greet(zpair, p)
    greet(zpair + 1, p)
    greet(yh * 16 + 2 * zother + c, p)
    greet(yflip, 2 * x + 1 - yl)
    greet(yflip + 1, 2 * x + 1 - yl)
    loads[1].start()
    raw_in_st[...] = jnp.zeros_like(raw_in_st)
    raw_out_st[...] = jnp.zeros_like(raw_out_st)
    raw_in_st[0:40, :] = tin_sh[...]
    raw_out_st[0:20, :] = tout_sh[...]
    pl.semaphore_wait(barrier, 20)

    for a, (st, raw) in enumerate(((raw_in_st, raw_in), (raw_out_st, raw_out))):
        remote(st, raw.at[c], raw_send.at[0, a], raw_recv.at[c, a], yflip + 1, 2 * x + 1 - yl).start()

        @pl.when(c == 0)
        def _():
            pltpu.make_async_copy(st, raw.at[0], raw_recv.at[0, a]).start()

        @pl.when(c != 0)
        def _():
            remote(st, raw.at[1], raw_send.at[1, a], raw_recv.at[1, a], fbase, p).start()
    yc = flip(yl, c)

    def send_wave(w):
        for n in range(4):
            xd = flip_x(x, n ^ (n >> 1))
            for hh in (1, 0):
                half = flip(c, hh)
                src = tok_hbm.at[xd, 4 * half + w]
                dst = xin.at[w, 2 * n + yc]
                arrive = tok_recv.at[w, 2 * n + yc]
                move = remote(src, dst, tok_send.at[w, 2 * n + hh], arrive, fbase + half, 2 * xd + c)
                if n == 0 and hh == 0:
                    @pl.when(yc == 0)
                    def _():
                        pltpu.make_async_copy(src, dst, arrive).start()

                    @pl.when(yc != 0)
                    def _():
                        move.start()
                else:
                    move.start()

    for w in range(4):
        send_wave(w)
    loads[0].start()
    loads[2].start()

    q_s[...] = jnp.zeros_like(q_s)
    k_s[0:4, :, HDIM:, :] = jnp.zeros((4, HEADS, 128 - HDIM, 128), BF)
    lane = lax.broadcasted_iota(jnp.int32, (128, 128), 1)
    ones = jnp.where(lane == HDIM, 1.0, 0.0).astype(BF)
    v_s[0:4] = jnp.broadcast_to(ones, (4, HEADS, 128, 128))
    rr = lax.broadcasted_iota(jnp.int32, (256, 256), 0)
    cc = lax.broadcasted_iota(jnp.int32, (256, 256), 1)
    bias[...] = jnp.where((rr % 8 == cc % 8) & (rr // 128 == cc // 128), 0.0, -1e30).astype(F32)

    yh_unit = flip(yh, c)
    toward = 1 - 2 * c

    def unit_at(offset):
        return yh_unit * 8 + (z + offset + 16) % 8

    def unit_refs(u):
        return (twin.at[pl.ds(pl.multiple_of(u * 80, 16), 80)], gout.at[u])

    lent = ((0, 1), (1, 1), (0, 2), (1, 2), (0, 4))

    def way_sign(way):
        return toward if way == 0 else -toward

    def ring(way, step):
        sign = way_sign(way)
        u = unit_at(-sign * (step - 1))
        frame = yh * 16 + 2 * ((z + sign + 8) % 8) + c
        return [
            remote(r, r, ring_send.at[way, step - 1, a], ring_recv.at[way, step - 1, a], frame, p)
            for a, r in enumerate(unit_refs(u))
        ]

    def ring_arrived(way, step):
        u = unit_at(-way_sign(way) * step)
        for a, r in enumerate(unit_refs(u)):
            wait_in(r, ring_recv.at[way, step - 1, a])
        return u

    def share(u, label):
        for a, r in enumerate(unit_refs(u)):
            remote(r, r, sib_send.at[label, a], sib_recv.at[label, a], sib, p).start()

    def weights_begin():
        for a, raw in enumerate((raw_in, raw_out)):
            wait_in(raw.at[0], raw_recv.at[0, a])
            wait_in(raw.at[1], raw_recv.at[1, a])
        u = unit_at(0)
        twin[pl.ds(pl.multiple_of(u * 80, 16), 80), :] = dot(
            pick(80, 96, 40, 48), raw_in[...].reshape(96, 1920)).astype(BF)
        gout[u] = dot(pick(48, 64, 20, 32), raw_out[...].reshape(64, 1280)).astype(BF)

        @pl.when(c == 0)
        def _():
            for way in (0, 1):
                for m in ring(way, 1):
                    m.start()

        share(u, 0)

    def weights_pass(way, step):
        u = ring_arrived(way, step)
        if step < 4 - way:
            for m in ring(way, step + 1):
                m.start()
        if (way, step) in lent:
            label = lent.index((way, step))
            for a, r in enumerate(unit_refs(u)):
                remote(r, r, lend_send.at[label, a], lend_recv.at[label, a], yflip + 1, 2 * x + 1 - yl).start()
        share(u, step if way == 0 else 4 + step)

    def weights_lent(label):
        way, step = lent[label]
        u = unit_at(-step if way == 0 else step)
        for a, r in enumerate(unit_refs(u)):
            wait_in(r, lend_recv.at[label, a])
        if step == 2:
            for m in ring(1 - way, 3):
                m.start()
        share(u, 8 + label)

    def core0(*moves):
        @pl.when(c == 0)
        def _():
            for way, step in moves:
                weights_pass(way, step)

    def core1(*moves):
        @pl.when(c == 1)
        def _():
            for label in moves:
                weights_lent(label)

    def labels(core):
        return [0, 1, 2, 3, 4, 5, 6, 7] if core == 0 else [0, 3, 7, 8, 9, 10, 11, 12]

    def weights_end():
        @pl.when(c == 1)
        def _():
            for way in (0, 1):
                share(ring_arrived(way, 3), 3 + 4 * way)
            weights_lent(4)

        other = flip(yh_unit, 1)
        for core in (0, 1):
            @pl.when(c != core)
            def _():
                for n, label in enumerate(labels(core)):
                    for a, r in enumerate(unit_refs(other * 8 + n)):
                        wait_in(r, sib_recv.at[label, a])
        twout[...] = dot(pick(640, 768, 40, 48), gout[...].reshape(768, 1280)).astype(BF)

    weights_begin()
    loads[1].wait()

    def chunk(w, carry):
        for s in range(8):
            wait_in(xin.at[w, s], tok_recv.at[w, s])
        rows = xin[w].reshape(128, D).astype(F32)
        normed = layer_norm(rows, sgain[...].reshape(1, D))
        pair = dot(normed, swin[:, INNER:]).astype(BF)
        keys = pair[:, 0:INNER].T
        for h in range(HEADS):
            lo = h * HDIM
            k_s[w, h, 0:HDIM, :] = keys[lo:lo + HDIM]
            v_s[w, h, :, 0:HDIM] = pair[:, INNER + lo:INNER + lo + HDIM]
        for a, r in enumerate((k_s, v_s)):
            remote(r.at[w], r.at[w + 4], kv_send.at[w, a], kv_recv.at[w, a], sib, p).start()
        queries = dot(normed, swin[:, 0:INNER]).astype(BF)
        for h in range(HEADS):
            q_s[h, w, :, 0:HDIM] = queries[:, h * HDIM:(h + 1) * HDIM]
        for after, moves0, moves1 in SERVICE:
            @pl.when(w == after)
            def _():
                core0(*moves0)
                core1(*moves1)

        return carry

    lax.fori_loop(0, 4, chunk, 0)
    for n in range(4):
        for a, r in enumerate((k_s, v_s)):
            wait_in(r.at[n + 4], kv_recv.at[n, a])

    def attend(w, count, first=0, last=HEADS):
        def head(h, carry):
            q = q_s[h, w:w + count].reshape(count * 128, 128)
            s = dot(q, jnp.concatenate([k_s[n, h] for n in range(8)], axis=1))
            top = jnp.max(s, axis=-1, keepdims=True)
            e = jnp.exp2((s - top) * EXP_SCALE).astype(BF)
            o = dot(e, v_s[:, h].reshape(1024, 128))
            o_s[h, 0:count * 128] = (o * (1.0 / o[:, HDIM:HDIM + 1])).astype(BF)
            return carry

        lax.fori_loop(first, last, head, 0, unroll=UNROLL)
        if last < HEADS:
            return
        mixed = jnp.concatenate([o_s[h, 0:count * 128, 0:HDIM] for h in range(HEADS)], axis=1)
        mx[w:w + count] = mixed.reshape(count, 8, 16, INNER)
        for v in range(w, w + count):
            for s in (7, 6, 5, 4, 3, 2, 1, 0):
                n, b = s // 2, s % 2
                patch = 2 * flip_x(x, n ^ (n >> 1)) + flip(yl, b)
                src, dst, arrive = mx.at[v, s], mback.at[v, c, x], mx_recv.at[v, c, x]
                move = remote(src, dst, mx_send.at[v, s], arrive, fbase + yl, patch)
                if s == 0:
                    @pl.when(yc == 0)
                    def _():
                        pltpu.make_async_copy(src, dst, arrive).start()

                    @pl.when(yc != 0)
                    def _():
                        move.start()
                else:
                    move.start()

    coef_space = keep[0, video].astype(F32) / KEEP
    coef_time = keep[1, video].astype(F32) / KEEP

    def to_video(w, src_buf, dst_buf, send, arrive):
        for k in (3, 2, 1, 0):
            o = 2 * flip(g // 2, k // 2) + flip(c, k % 2)
            src, dst = src_buf.at[w, o], dst_buf.at[w, g]
            if k == 0:
                pltpu.make_async_copy(src, dst, arrive.at[w, g]).start()
            else:
                remote(src, dst, send.at[w, k], arrive.at[w, g], 4 * video + o, p).start()

    def after_space(w):
        for h in range(2):
            for i in range(4):
                wait_in(mback.at[w, h, i], mx_recv.at[w, h, i])
        y = dot(mback[w].reshape(128, INNER), swout[...]) * coef_space
        for h in range(2):
            rows = [tok[i, 4 * h + w].astype(F32) + y[(4 * h + i) * 16:(4 * h + i + 1) * 16] for i in range(4)]
            for core in range(2):
                asp[w, 2 * h + core] = jnp.concatenate([r[8 * core:8 * core + 8] for r in rows], axis=0).astype(BF)
        to_video(w, asp, tin, as_send, as_recv)

    def temporal(w, count):
        for v in range(w, w + count):
            for o in range(4):
                wait_in(tin.at[v, o], as_recv.at[v, o])
        size = count * 128
        rows = tin[w:w + count].reshape(size, D).astype(F32)
        triple = dot(layer_norm(rows, tgain[...].reshape(1, D)), twin[...]).astype(BF)
        parts = []
        for h in range(HEADS):
            lo = h * HDIM
            s = dot_t(triple[:, lo:lo + HDIM], triple[:, INNER + lo:INNER + lo + HDIM]) + bias[0:size, 0:size]
            top = jnp.max(s, axis=-1, keepdims=True)
            e = jnp.exp2((s - top) * EXP_SCALE)
            total = jnp.sum(e, axis=-1, keepdims=True)
            o = dot(e.astype(BF), triple[:, 2 * INNER + lo:2 * INNER + lo + HDIM])
            parts.append((o * (1.0 / total)).astype(BF))
        tm[w:w + count] = jnp.concatenate(parts, axis=1).reshape(count, 4, 32, INNER)
        for v in range(w, w + count):
            to_video(v, tm, tb, tm_send, tm_recv)

    def finish(w, count):
        for v in range(w, w + count):
            for o in range(4):
                wait_in(tb.at[v, o], tm_recv.at[v, o])
        y = dot(tb[w:w + count].reshape(count * 128, INNER), twout[...]) * coef_time
        for v in range(w, w + count):
            for h in range(2):
                low, high = [
                    asp[v, 2 * h + core].astype(F32)
                    + y[((v - w) * 4 + 2 * h + core) * 32:((v - w) * 4 + 2 * h + core + 1) * 32]
                    for core in range(2)]
                for i in range(4):
                    out_v[i, 4 * h + v] = jnp.concatenate(
                        [low[8 * i:8 * i + 8], high[8 * i:8 * i + 8]], axis=0).astype(BF)
            for h in range(2):
                pltpu.make_async_copy(out_v.at[:, 4 * h + v], out_hbm.at[:, 4 * h + v], out_sem.at[v, h]).start()

    loads[0].wait()
    loads[2].wait()
    for move, *what in PLAN:
        {'attend': attend, 'after': after_space, 'temporal': temporal, 'finish': finish,
         'core0': core0, 'core1': core1, 'end': weights_end}[move](*what)

    for w in range(4):
        part = tok_hbm.at[0, 0]
        for s in range(8):
            if s == 0:
                @pl.when(yc != 0)
                def _():
                    wait_out(part, tok_send.at[w, 0])
                    wait_out(mx.at[w, 0], mx_send.at[w, 0])
            else:
                wait_out(part, tok_send.at[w, s])
                wait_out(mx.at[w, s], mx_send.at[w, s])
        for a, r in enumerate((k_s, v_s)):
            wait_out(r.at[w], kv_send.at[w, a])
        for k in range(1, 4):
            wait_out(asp.at[w, k], as_send.at[w, k])
            wait_out(tm.at[w, k], tm_send.at[w, k])
    for a, st in enumerate((raw_in_st, raw_out_st)):
        wait_out(st, raw_send.at[0, a])

        @pl.when(c != 0)
        def _():
            wait_out(st, raw_send.at[1, a])
    for a, r in enumerate(unit_refs(0)):
        for core in (0, 1):
            @pl.when(c == core)
            def _():
                for way in range(2):
                    for step in (range(4 - way) if core == 0 else (2,)):
                        wait_out(r, ring_send.at[way, step, a])
                for label in labels(core):
                    wait_out(r, sib_send.at[label, a])
                if core == 0:
                    for label in range(len(lent)):
                        wait_out(r, lend_send.at[label, a])
    for w in range(4):
        for h in range(2):
            pltpu.make_async_copy(out_v.at[:, 4 * h + w], out_hbm.at[:, 4 * h + w], out_sem.at[w, h]).wait()


def on_device(tokens, spatial_in, spatial_out, temporal_in, temporal_out, spatial_gain, temporal_gain, keep_masks):
    dma = pltpu.SemaphoreType.DMA
    scratch = [
        pltpu.VMEM((4, 8, 16, D), BF),
        pltpu.VMEM((D, 3 * INNER), BF),
        pltpu.VMEM((INNER, D), BF),
        pltpu.VMEM((D, 3 * INNER), BF),
        pltpu.VMEM((16, 48, D), BF),
        pltpu.VMEM((INNER, D), BF),
        pltpu.VMEM((48, 3 * INNER), BF),
        pltpu.VMEM((32, D), BF),
        pltpu.VMEM((2, 48, 3 * INNER), BF),
        pltpu.VMEM((2, 32, D), BF),
        pltpu.VMEM((4, 8, 16, D), BF),
        pltpu.VMEM((HEADS, 4, 128, 128), BF),
        pltpu.VMEM((8, HEADS, 128, 128), BF),
        pltpu.VMEM((8, HEADS, 128, 128), BF),
        pltpu.VMEM((HEADS, 256, 128), BF),
        pltpu.VMEM((4, 8, 16, INNER), BF),
        pltpu.VMEM((4, 2, 4, 16, INNER), BF),
        pltpu.VMEM((4, 4, 32, D), BF),
        pltpu.VMEM((4, 4, 32, D), BF),
        pltpu.VMEM((4, 4, 32, INNER), BF),
        pltpu.VMEM((4, 4, 32, INNER), BF),
        pltpu.VMEM((4, 8, 16, D), BF),
        pltpu.VMEM((256, 256), F32),
        dma((3,)), dma((4, 8)), dma((4, 8)), dma((4, 2)), dma((4, 2)), dma((4, 8)), dma((4, 2, 4)),
        dma((4, 4)), dma((4, 4)), dma((4, 4)), dma((4, 4)), dma((2, 2)), dma((2, 2)),
        dma((2, 4, 2)), dma((2, 4, 2)), dma((13, 2)), dma((13, 2)), dma((5, 2)), dma((5, 2)), dma((4, 2)),
    ]
    any_space = pl.BlockSpec(memory_space=pl.ANY)
    vmem = pl.BlockSpec(memory_space=pltpu.VMEM)
    out = pl.pallas_call(
        layer,
        out_shape=jax.ShapeDtypeStruct((4, 8, 16, D), BF),
        in_specs=[any_space, any_space, any_space, vmem, vmem, vmem, vmem,
                  pl.BlockSpec(memory_space=pltpu.SMEM)],
        out_specs=any_space,
        scratch_shapes=scratch,
        compiler_params=pltpu.CompilerParams(
            collective_id=0, has_side_effects=True, vmem_limit_bytes=60 * 1024 * 1024),
    )(tokens.reshape(4, 8, 16, D), spatial_in, spatial_out, temporal_in, temporal_out,
      spatial_gain, temporal_gain, keep_masks.T)
    return out.reshape(4, 128, D)


def solution(mesh):
    placed = (
        P("frame", "patch", None), P(), P(), P("frame", None), P("frame", None), P(), P(), P(),
    )
    return jax.shard_map(
        on_device, mesh=mesh, in_specs=placed, out_specs=P("frame", "patch", None), check_vma=False)
```

```python
import jax
import jax.numpy as jnp
from jax import lax
from jax.experimental import pallas as pl
from jax.experimental.pallas import tpu as pltpu
from jax.sharding import PartitionSpec as P

MESH = pl.DeviceIdType.MESH
BF = jnp.bfloat16
F32 = jnp.float32

HEADS = 8
HDIM = 80
INNER = HEADS * HDIM
D = 1280
KEEP = 0.7
UNROLL = 4
SERVICE = ((0, ((0, 1), (1, 1)), ()), (2, ((0, 2), (1, 2)), ((1, True),)))
PLAN = (
    ('attend', 0, 1),
    ('core0', (0, 3), (1, 3)),
    ('core1', (1, False), (2, True)),
    ('attend', 1, 1),
    ('after', 0),
    ('attend', 2, 1),
    ('after', 1),
    ('core0', (0, 4)),
    ('core1', (2, False), (3, True)),
    ('attend', 3, 1),
    ('after', 2),
    ('after', 3),
    ('core1', (3, False)),
    ('end',),
    ('temporal', 0, 2),
    ('temporal', 2, 2),
    ('out',),
    ('finish', 0, 2),
    ('finish', 2, 2),
)
EXP_SCALE = HDIM ** (-0.5) * 1.4426950408889634


def flip(a, b):
    return (a + b) % 2


def flip_x(x, key):
    low, high = x % 2, x // 2
    if key % 2:
        low = 1 - low
    if key // 2:
        high = 1 - high
    return 2 * high + low


def layer_norm(x, gain):
    center = jnp.sum(x, axis=-1, keepdims=True) * (1.0 / D)
    x = x - center
    spread = jnp.sum(x * x, axis=-1, keepdims=True) * (1.0 / D)
    return (x * lax.rsqrt(spread + 1e-06) * gain).astype(BF)


def dot(a, b):
    return jnp.dot(a, b, preferred_element_type=F32)


def dot_t(a, b):
    return lax.dot_general(a, b, (((1,), (1,)), ((), ())), preferred_element_type=F32)


def pick(rows, columns, group, stride):
    r = lax.broadcasted_iota(jnp.int32, (rows, columns), 0)
    c = lax.broadcasted_iota(jnp.int32, (rows, columns), 1)
    block = jnp.zeros_like(r)
    for n in range(1, (rows + group - 1) // group):
        block = block + (r >= n * group).astype(jnp.int32)
    hit = (c == r + block * (stride - group)) & (r < group * (columns // stride))
    return jnp.where(hit, 1.0, 0.0).astype(BF)


def layer(
    tok_hbm, swin_hbm, swout_hbm, tin_sh, tout_sh, sgain, tgain, keep, out_hbm,
    tok, swin, swout, twin, gout, twout, raw_in_st, raw_out_st, raw_in, raw_out,
    xin, q_s, k_s, v_s, o_s, mx, mback, asp, tin, tm, tb, out_v, bias,
    load_sem, tok_send, tok_recv, kv_send, kv_recv, mx_send, mx_recv,
    as_send, as_recv, tm_send, tm_recv, raw_send, raw_recv,
    ring_send, ring_recv, sib_send, sib_recv, lend_send, lend_recv, out_sem,
):
    f = lax.axis_index("frame")
    p = lax.axis_index("patch")
    c = f % 2
    z = (f // 2) % 8
    yh = f // 16
    x = p // 2
    yl = p % 2
    fbase = f - c
    video = f // 4
    g = f % 4
    zb = z % 2
    sib = fbase + 1 - c

    def remote(src, dst, send, recv, frame, patch):
        return pltpu.make_async_remote_copy(
            src_ref=src, dst_ref=dst, send_sem=send, recv_sem=recv,
            device_id=(frame, patch), device_id_type=MESH)

    def wait_in(dst, sem):
        pltpu.make_async_copy(dst, dst, sem).wait()

    wait_out = wait_in

    loads = [
        pltpu.make_async_copy(tok_hbm, tok, load_sem.at[0]),
        pltpu.make_async_copy(swin_hbm, swin, load_sem.at[1]),
        pltpu.make_async_copy(swout_hbm, swout, load_sem.at[2]),
    ]

    barrier = pltpu.get_barrier_semaphore()

    def greet(frame, patch):
        pl.semaphore_signal(barrier, inc=1, device_id=(frame, patch), device_id_type=MESH)

    zother = (z + 7 + 2 * zb) % 8
    yflip = (f + 16) % 32 - c
    for n in range(4):
        for b in range(2):
            patch = 2 * flip_x(x, n) + flip(yl, b)
            greet(sib, patch)
            if n or b:
                greet(f, patch)
    zpair = (f - g) + 2 * (1 - zb)
    greet(zpair, p)
    greet(zpair + 1, p)
    greet(yh * 16 + 2 * zother + c, p)
    greet(yflip, 2 * x + 1 - yl)
    greet(yflip + 1, 2 * x + 1 - yl)
    loads[1].start()
    raw_in_st[...] = jnp.zeros_like(raw_in_st)
    raw_out_st[...] = jnp.zeros_like(raw_out_st)
    raw_in_st[0:40, :] = tin_sh[...]
    raw_out_st[0:20, :] = tout_sh[...]
    pl.semaphore_wait(barrier, 20)

    for a, (st, raw) in enumerate(((raw_in_st, raw_in), (raw_out_st, raw_out))):
        remote(st, raw.at[c], raw_send.at[0, a], raw_recv.at[c, a], yflip + 1, 2 * x + 1 - yl).start()

        @pl.when(c == 0)
        def _():
            pltpu.make_async_copy(st, raw.at[0], raw_recv.at[0, a]).start()

        @pl.when(c != 0)
        def _():
            remote(st, raw.at[1], raw_send.at[1, a], raw_recv.at[1, a], fbase, p).start()
    yc = flip(yl, c)

    def send_wave(w):
        for n in range(4):
            xd = flip_x(x, n ^ (n >> 1))
            for hh in (1, 0):
                half = flip(c, hh)
                src = tok_hbm.at[xd, 4 * half + w]
                dst = xin.at[w, 2 * n + yc]
                arrive = tok_recv.at[w, 2 * n + yc]
                move = remote(src, dst, tok_send.at[w, 2 * n + hh], arrive, fbase + half, 2 * xd + c)
                if n == 0 and hh == 0:
                    @pl.when(yc == 0)
                    def _():
                        pltpu.make_async_copy(src, dst, arrive).start()

                    @pl.when(yc != 0)
                    def _():
                        move.start()
                else:
                    move.start()

    for w in range(4):
        send_wave(w)
    loads[0].start()
    loads[2].start()

    q_s[...] = jnp.zeros_like(q_s)
    k_s[0:4, :, HDIM:, :] = jnp.zeros((4, HEADS, 128 - HDIM, 128), BF)
    lane = lax.broadcasted_iota(jnp.int32, (128, 128), 1)
    ones = jnp.where(lane == HDIM, 1.0, 0.0).astype(BF)
    v_s[0:4] = jnp.broadcast_to(ones, (4, HEADS, 128, 128))
    rr = lax.broadcasted_iota(jnp.int32, (256, 256), 0)
    cc = lax.broadcasted_iota(jnp.int32, (256, 256), 1)
    bias[...] = jnp.where((rr % 8 == cc % 8) & (rr // 128 == cc // 128), 0.0, -1e30).astype(F32)

    yh_unit = flip(yh, c)
    toward = 1 - 2 * c

    def unit_at(offset):
        return yh_unit * 8 + (z + offset + 16) % 8

    def unit_refs(u):
        return (twin.at[pl.ds(pl.multiple_of(u * 80, 16), 80)], gout.at[u])

    odd = x % 2

    def way_sign(way):
        return toward if way == 0 else -toward

    def ring(way, step):
        sign = way_sign(way)
        u = unit_at(-sign * (step - 1))
        frame = yh * 16 + 2 * ((z + sign + 8) % 8) + c
        return [
            remote(r, r, ring_send.at[way, step - 1, a], ring_recv.at[way, step - 1, a], frame, p)
            for a, r in enumerate(unit_refs(u))
        ]

    def ring_arrived(way, step):
        u = unit_at(-way_sign(way) * step)
        for a, r in enumerate(unit_refs(u)):
            wait_in(r, ring_recv.at[way, step - 1, a])
        return u

    def share(u, label):
        for a, r in enumerate(unit_refs(u)):
            remote(r, r, sib_send.at[label, a], sib_recv.at[label, a], sib, p).start()

    def weights_begin():
        for a, raw in enumerate((raw_in, raw_out)):
            wait_in(raw.at[0], raw_recv.at[0, a])
            wait_in(raw.at[1], raw_recv.at[1, a])
        u = unit_at(0)
        twin[pl.ds(pl.multiple_of(u * 80, 16), 80), :] = dot(
            pick(80, 96, 40, 48), raw_in[...].reshape(96, 1920)).astype(BF)
        gout[u] = dot(pick(48, 64, 20, 32), raw_out[...].reshape(64, 1280)).astype(BF)

        @pl.when(c == 0)
        def _():
            for way in (0, 1):
                for m in ring(way, 1):
                    m.start()

        share(u, 0)

    def weights_pass(way, step):
        u = ring_arrived(way, step)
        if step < 4 - way:
            for m in ring(way, step + 1):
                m.start()
        label = 2 * (step - 1) + way

        @pl.when((odd == way) | (step == 4))
        def _():
            for a, r in enumerate(unit_refs(u)):
                remote(r, r, lend_send.at[label, a], lend_recv.at[label, a], yflip + 1, 2 * x + 1 - yl).start()

        share(u, step if way == 0 else 4 + step)

    def weights_lent(step, direct):
        way = odd if direct else 1 - odd
        u = unit_at(step * (2 * way - 1))
        label = 2 * (step - 1) + way
        for a, r in enumerate(unit_refs(u)):
            wait_in(r, lend_recv.at[label, a])
            if direct:
                remote(r, r, lend_send.at[label, a], lend_recv.at[label, a], f, 2 * flip_x(x, 1) + yl).start()
        share(u, 8 + label)

    def core0(*moves):
        @pl.when(c == 0)
        def _():
            for way, step in moves:
                weights_pass(way, step)

    def core1(*moves):
        @pl.when(c == 1)
        def _():
            for move in moves:
                weights_lent(*move)

    def labels(core):
        return [0, 1, 2, 3, 4, 5, 6, 7] if core == 0 else [0, 8, 9, 10, 11, 12, 13, 14]

    def weights_end():
        @pl.when(c == 1)
        def _():
            u = unit_at(4)
            for a, r in enumerate(unit_refs(u)):
                wait_in(r, lend_recv.at[6, a])
            share(u, 14)

        other = flip(yh_unit, 1)
        for core in (0, 1):
            @pl.when(c != core)
            def _():
                for n, label in enumerate(labels(core)):
                    for a, r in enumerate(unit_refs(other * 8 + n)):
                        wait_in(r, sib_recv.at[label, a])

    def weights_out():
        twout[...] = dot(pick(640, 768, 40, 48), gout[...].reshape(768, 1280)).astype(BF)

    weights_begin()
    loads[1].wait()

    def chunk(w, carry):
        for s in range(8):
            wait_in(xin.at[w, s], tok_recv.at[w, s])
        rows = xin[w].reshape(128, D).astype(F32)
        normed = layer_norm(rows, sgain[...].reshape(1, D))
        pair = dot(normed, swin[:, INNER:]).astype(BF)
        keys = pair[:, 0:INNER].T
        for h in range(HEADS):
            lo = h * HDIM
            k_s[w, h, 0:HDIM, :] = keys[lo:lo + HDIM]
            v_s[w, h, :, 0:HDIM] = pair[:, INNER + lo:INNER + lo + HDIM]
        for a, r in enumerate((k_s, v_s)):
            remote(r.at[w], r.at[w + 4], kv_send.at[w, a], kv_recv.at[w, a], sib, p).start()
        queries = dot(normed, swin[:, 0:INNER]).astype(BF)
        for h in range(HEADS):
            q_s[h, w, :, 0:HDIM] = queries[:, h * HDIM:(h + 1) * HDIM]
        for after, moves0, moves1 in SERVICE:
            @pl.when(w == after)
            def _():
                core0(*moves0)
                core1(*moves1)

        return carry

    lax.fori_loop(0, 4, chunk, 0)
    for n in range(4):
        for a, r in enumerate((k_s, v_s)):
            wait_in(r.at[n + 4], kv_recv.at[n, a])

    def attend(w, count, first=0, last=HEADS):
        def head(h, carry):
            q = q_s[h, w:w + count].reshape(count * 128, 128)
            s = dot(q, jnp.concatenate([k_s[n, h] for n in range(8)], axis=1))
            top = jnp.max(s, axis=-1, keepdims=True)
            e = jnp.exp2((s - top) * EXP_SCALE).astype(BF)
            o = dot(e, v_s[:, h].reshape(1024, 128))
            o_s[h, 0:count * 128] = (o * (1.0 / o[:, HDIM:HDIM + 1])).astype(BF)
            return carry

        lax.fori_loop(first, last, head, 0, unroll=UNROLL)
        if last < HEADS:
            return
        mixed = jnp.concatenate([o_s[h, 0:count * 128, 0:HDIM] for h in range(HEADS)], axis=1)
        mx[w:w + count] = mixed.reshape(count, 8, 16, INNER)
        for v in range(w, w + count):
            for s in (7, 6, 5, 4, 3, 2, 1, 0):
                n, b = s // 2, s % 2
                patch = 2 * flip_x(x, n ^ (n >> 1)) + flip(yl, b)
                src, dst, arrive = mx.at[v, s], mback.at[v, c, x], mx_recv.at[v, c, x]
                move = remote(src, dst, mx_send.at[v, s], arrive, fbase + yl, patch)
                if s == 0:
                    @pl.when(yc == 0)
                    def _():
                        pltpu.make_async_copy(src, dst, arrive).start()

                    @pl.when(yc != 0)
                    def _():
                        move.start()
                else:
                    move.start()

    coef_space = keep[0, video].astype(F32) / KEEP
    coef_time = keep[1, video].astype(F32) / KEEP

    def to_video(w, src_buf, dst_buf, send, arrive):
        for k in (3, 2, 1, 0):
            o = 2 * flip(g // 2, k // 2) + flip(c, k % 2)
            src, dst = src_buf.at[w, o], dst_buf.at[w, g]
            if k == 0:
                pltpu.make_async_copy(src, dst, arrive.at[w, g]).start()
            else:
                remote(src, dst, send.at[w, k], arrive.at[w, g], 4 * video + o, p).start()

    def after_space(w):
        for h in range(2):
            for i in range(4):
                wait_in(mback.at[w, h, i], mx_recv.at[w, h, i])
        y = dot(mback[w].reshape(128, INNER), swout[...]) * coef_space
        for h in range(2):
            rows = [tok[i, 4 * h + w].astype(F32) + y[(4 * h + i) * 16:(4 * h + i + 1) * 16] for i in range(4)]
            for core in range(2):
                asp[w, 2 * h + core] = jnp.concatenate([r[8 * core:8 * core + 8] for r in rows], axis=0).astype(BF)
        to_video(w, asp, tin, as_send, as_recv)

    def temporal(w, count):
        for v in range(w, w + count):
            for o in range(4):
                wait_in(tin.at[v, o], as_recv.at[v, o])
        size = count * 128
        rows = tin[w:w + count].reshape(size, D).astype(F32)
        triple = dot(layer_norm(rows, tgain[...].reshape(1, D)), twin[...]).astype(BF)
        parts = []
        for h in range(HEADS):
            lo = h * HDIM
            s = dot_t(triple[:, lo:lo + HDIM], triple[:, INNER + lo:INNER + lo + HDIM]) + bias[0:size, 0:size]
            top = jnp.max(s, axis=-1, keepdims=True)
            e = jnp.exp2((s - top) * EXP_SCALE)
            total = jnp.sum(e, axis=-1, keepdims=True)
            o = dot(e.astype(BF), triple[:, 2 * INNER + lo:2 * INNER + lo + HDIM])
            parts.append((o * (1.0 / total)).astype(BF))
        tm[w:w + count] = jnp.concatenate(parts, axis=1).reshape(count, 4, 32, INNER)
        for v in range(w, w + count):
            to_video(v, tm, tb, tm_send, tm_recv)

    def finish(w, count):
        for v in range(w, w + count):
            for o in range(4):
                wait_in(tb.at[v, o], tm_recv.at[v, o])
        y = dot(tb[w:w + count].reshape(count * 128, INNER), twout[...]) * coef_time
        for v in range(w, w + count):
            for h in range(2):
                low, high = [
                    asp[v, 2 * h + core].astype(F32)
                    + y[((v - w) * 4 + 2 * h + core) * 32:((v - w) * 4 + 2 * h + core + 1) * 32]
                    for core in range(2)]
                for i in range(4):
                    out_v[i, 4 * h + v] = jnp.concatenate(
                        [low[8 * i:8 * i + 8], high[8 * i:8 * i + 8]], axis=0).astype(BF)
            for h in range(2):
                pltpu.make_async_copy(out_v.at[:, 4 * h + v], out_hbm.at[:, 4 * h + v], out_sem.at[v, h]).start()

    loads[0].wait()
    loads[2].wait()
    for move, *what in PLAN:
        {'attend': attend, 'after': after_space, 'temporal': temporal, 'finish': finish,
         'core0': core0, 'core1': core1, 'end': weights_end,
         'out': weights_out}[move](*what)

    for w in range(4):
        part = tok_hbm.at[0, 0]
        for s in range(8):
            if s == 0:
                @pl.when(yc != 0)
                def _():
                    wait_out(part, tok_send.at[w, 0])
                    wait_out(mx.at[w, 0], mx_send.at[w, 0])
            else:
                wait_out(part, tok_send.at[w, s])
                wait_out(mx.at[w, s], mx_send.at[w, s])
        for a, r in enumerate((k_s, v_s)):
            wait_out(r.at[w], kv_send.at[w, a])
        for k in range(1, 4):
            wait_out(asp.at[w, k], as_send.at[w, k])
            wait_out(tm.at[w, k], tm_send.at[w, k])
    for a, st in enumerate((raw_in_st, raw_out_st)):
        wait_out(st, raw_send.at[0, a])

        @pl.when(c != 0)
        def _():
            wait_out(st, raw_send.at[1, a])
    for a, r in enumerate(unit_refs(0)):
        for core in (0, 1):
            @pl.when(c == core)
            def _():
                for way in range(2):
                    for step in range(4 - way if core == 0 else 0):
                        wait_out(r, ring_send.at[way, step, a])
                for label in labels(core):
                    wait_out(r, sib_send.at[label, a])
                if core == 0:
                    wait_out(r, lend_send.at[6, a])
        for step in range(3):
            wait_out(r, lend_send.at[2 * step + odd, a])
    for w in range(4):
        for h in range(2):
            pltpu.make_async_copy(out_v.at[:, 4 * h + w], out_hbm.at[:, 4 * h + w], out_sem.at[w, h]).wait()


def on_device(tokens, spatial_in, spatial_out, temporal_in, temporal_out, spatial_gain, temporal_gain, keep_masks):
    dma = pltpu.SemaphoreType.DMA
    scratch = [
        pltpu.VMEM((4, 8, 16, D), BF),
        pltpu.VMEM((D, 3 * INNER), BF),
        pltpu.VMEM((INNER, D), BF),
        pltpu.VMEM((D, 3 * INNER), BF),
        pltpu.VMEM((16, 48, D), BF),
        pltpu.VMEM((INNER, D), BF),
        pltpu.VMEM((48, 3 * INNER), BF),
        pltpu.VMEM((32, D), BF),
        pltpu.VMEM((2, 48, 3 * INNER), BF),
        pltpu.VMEM((2, 32, D), BF),
        pltpu.VMEM((4, 8, 16, D), BF),
        pltpu.VMEM((HEADS, 4, 128, 128), BF),
        pltpu.VMEM((8, HEADS, 128, 128), BF),
        pltpu.VMEM((8, HEADS, 128, 128), BF),
        pltpu.VMEM((HEADS, 256, 128), BF),
        pltpu.VMEM((4, 8, 16, INNER), BF),
        pltpu.VMEM((4, 2, 4, 16, INNER), BF),
        pltpu.VMEM((4, 4, 32, D), BF),
        pltpu.VMEM((4, 4, 32, D), BF),
        pltpu.VMEM((4, 4, 32, INNER), BF),
        pltpu.VMEM((4, 4, 32, INNER), BF),
        pltpu.VMEM((4, 8, 16, D), BF),
        pltpu.VMEM((256, 256), F32),
        dma((3,)), dma((4, 8)), dma((4, 8)), dma((4, 2)), dma((4, 2)), dma((4, 8)), dma((4, 2, 4)),
        dma((4, 4)), dma((4, 4)), dma((4, 4)), dma((4, 4)), dma((2, 2)), dma((2, 2)),
        dma((2, 4, 2)), dma((2, 4, 2)), dma((15, 2)), dma((15, 2)), dma((7, 2)), dma((7, 2)), dma((4, 2)),
    ]
    any_space = pl.BlockSpec(memory_space=pl.ANY)
    vmem = pl.BlockSpec(memory_space=pltpu.VMEM)
    out = pl.pallas_call(
        layer,
        out_shape=jax.ShapeDtypeStruct((4, 8, 16, D), BF),
        in_specs=[any_space, any_space, any_space, vmem, vmem, vmem, vmem,
                  pl.BlockSpec(memory_space=pltpu.SMEM)],
        out_specs=any_space,
        scratch_shapes=scratch,
        compiler_params=pltpu.CompilerParams(
            collective_id=0, has_side_effects=True, vmem_limit_bytes=60 * 1024 * 1024),
    )(tokens.reshape(4, 8, 16, D), spatial_in, spatial_out, temporal_in, temporal_out,
      spatial_gain, temporal_gain, keep_masks.T)
    return out.reshape(4, 128, D)


def solution(mesh):
    placed = (
        P("frame", "patch", None), P(), P(), P("frame", None), P("frame", None), P(), P(), P(),
    )
    return jax.shard_map(
        on_device, mesh=mesh, in_specs=placed, out_specs=P("frame", "patch", None), check_vma=False)
```
